128 devices in a mesh: cell: 64 (over z, x, y_lo, core), rcv: 2 (over y_hi).
Axes of the slice: x: 4, y: 4 (y_hi: 2, y_lo: 2; y = y_hi * 2 + y_lo), z: 4, core: 2. Of those that a mesh axis runs over, the one named last changes fastest.
Arguments:
- green: float32 [1024, 131072], P('rcv', 'cell'), may hold values from -0.015625 to 0.015625
- field: float32 [131072, 512], P('cell'), may hold values from -6 to 6
- probe: float32 [4, 131072], P(None, 'cell'), may hold values from -6 to 6
- cov_inv: float32 [1024, 1024], P('rcv'), as said below
Outputs:
- hessian: float32 [4, 131072], P(None, 'cell')
- curvature: float32 [4, 4], replicated
The draws below stay inside these ranges and needn't reach their ends.
Inputs may be any that keep to these rules, and one draw needn't show every extreme that they name: `cov_inv`: symmetric positive definite.
All inputs are finite; a program needn't handle non-finite values.
Results may differ from the reference program's by a relative error of at most 0.0001.
Values sent between devices are 32-bit elements; how exact they have to be, the bound alone decides.
A program may use at most 128 MiB of HBM per device.

```python
import jax
import jax.numpy as jnp
from jax import lax

RECEIVER_COUNT = 1024
SOURCE_COUNT = 512
PROBE_COUNT = 4
CELL_DEV = 2048
CELLS = 131072


def draw_cov_inv(key, part):
    base = jax.random.fold_in(key, 11)
    key_mix, key_diag = jax.random.split(base)
    mixing_matrix = jax.random.normal(key_mix, (RECEIVER_COUNT, RECEIVER_COUNT), jnp.float32) * (0.5 / RECEIVER_COUNT ** 0.5)
    levels = jnp.exp(jax.random.uniform(key_diag, (RECEIVER_COUNT,), jnp.float32) * jnp.log(2.0))
    matrix = jnp.dot(mixing_matrix, mixing_matrix.T, precision=lax.Precision.HIGHEST) + jnp.diag(levels)
    return matrix


def block_levels(own_key, shape, cuts, low, top_value):
    gain = 1.0
    for axis_at, parts in cuts:
        heights = jax.random.uniform(jax.random.fold_in(jax.random.fold_in(own_key, 6), axis_at), (parts,), jnp.float32, low / len(cuts), top_value / len(cuts))
        gain = gain * jnp.repeat(jnp.exp(heights), shape[axis_at] // parts).reshape((-1,) + (1,) * (len(shape) - 1 - axis_at))
    return gain


def gaussian(rng, dims, spread, bound, cuts=(), kind=jnp.bfloat16):
    values = jax.random.normal(rng, dims, jnp.float32) * spread
    if len(cuts) > 0:
        values = block_levels(rng, dims, cuts, -0.22, 0.18) * values
    return jnp.clip(values, min=-bound, max=bound).astype(kind)


def setup_inputs(seed: int = 0) -> dict:
    key_list = jax.random.split(jax.random.key(seed), 5)
    return {
        "green": gaussian(key_list[0], (RECEIVER_COUNT, CELLS), CELLS ** -0.5, 0.015625, ((0, 2), (1, 64)), jnp.float32),
        "field": gaussian(key_list[1], (CELLS, SOURCE_COUNT), 1.0, 6.0, ((0, 64),), jnp.float32),
        "probe": gaussian(key_list[2], (PROBE_COUNT, CELLS), 1.0, 6.0, ((1, 64),), jnp.float32),
        "cov_inv": draw_cov_inv(jax.random.fold_in(key_list[4], 71), 0),
    }


def reference(green, field, probe, cov_inv):
    highest_precision = lax.Precision.HIGHEST
    sensitivity_blocks = CELLS // CELL_DEV
    g_blocks = green.reshape(RECEIVER_COUNT, sensitivity_blocks, CELL_DEV).transpose(1, 0, 2)
    f_blocks = field.reshape(sensitivity_blocks, CELL_DEV, SOURCE_COUNT)
    p_blocks = probe.reshape(PROBE_COUNT, sensitivity_blocks, CELL_DEV).transpose(1, 0, 2)

    def forward(total, pieces):
        g_part, f_part, p_part = pieces
        lifted = (f_part[:, :, None] * p_part.T[:, None, :]).reshape(CELL_DEV, SOURCE_COUNT * PROBE_COUNT)
        return total + jnp.dot(g_part, lifted, precision=highest_precision, preferred_element_type=jnp.float32), None

    measured_data, _ = lax.scan(forward, jnp.zeros((RECEIVER_COUNT, SOURCE_COUNT * PROBE_COUNT), jnp.float32), (g_blocks, f_blocks, p_blocks))
    whitened_data = jnp.dot(cov_inv, measured_data, precision=highest_precision, preferred_element_type=jnp.float32)
    curvature = jnp.einsum("dou,dob->ub", measured_data.reshape(RECEIVER_COUNT, SOURCE_COUNT, PROBE_COUNT), whitened_data.reshape(RECEIVER_COUNT, SOURCE_COUNT, PROBE_COUNT), precision=highest_precision) / (RECEIVER_COUNT * SOURCE_COUNT)

    def backward(pieces):
        g_part, f_part = pieces
        back = jnp.dot(g_part.T, whitened_data, precision=highest_precision, preferred_element_type=jnp.float32).reshape(CELL_DEV, SOURCE_COUNT, PROBE_COUNT)
        return jnp.einsum("cs,csp->pc", f_part, back, precision=highest_precision)

    hess = lax.map(backward, (g_blocks, f_blocks))
    hessian = hess.transpose(1, 0, 2).reshape(PROBE_COUNT, CELLS)
    return hessian, curvature
```

```python
import functools

import jax
import jax.numpy as jnp
from jax import lax
from jax.experimental import pallas as pl
from jax.experimental.pallas import tpu as pltpu
from jax.sharding import PartitionSpec as P

MESH = pl.DeviceIdType.MESH
F32 = jnp.float32
BF16 = jnp.bfloat16
NP = 4
S = 512
R = 512
C = 2048
KB = 512
NKB = C // KB
NB = 512
NNB = C // NB

ORDER = """F1.0 F0.0 C.0 F1.1 F0.1 C.1 F1.2 A.0 F0.2 C.2 F1.3 A.1 Y.0 F0.3 C.3
A.2 R.0 Y.1 A.3 R.1 Y.2 V.0 U.0 R.2 Y.3 V.1 B0.0 U.1 R.3 G0 V.2 B1.0 U.2 B0.1 V.3 G1 B1.1 U.3 G2 B0.2 G3 B1.2
B0.3 B1.3""".split()


def flip(v, m):
    if m == 0:
        return v
    if m == 1:
        return v + 1 - 2 * lax.rem(v, 2)
    if m == 2:
        return lax.rem(v + 2, 4)
    return 3 - v


def split(a):
    hi = a.astype(BF16)
    return hi, (a - hi.astype(F32)).astype(BF16)


def nt(a, b):
    return lax.dot_general(a, b, (((1,), (1,)), ((), ())), preferred_element_type=F32)


def nn(a, b):
    return lax.dot_general(a, b, (((1,), (0,)), ((), ())), preferred_element_type=F32)


def kernel(order, green, field, probe, cov, h_out, hr_out, g_out,
           graw, fraw, craw, prb, ghi, glo, ft, chi, clo, data, core_in, ring_in, pair_in, own, far, white, hess,
           gram, g8, g4, g2, g1, lsem, ssem, rsem):
    cell = lax.axis_index("cell")
    rcv = lax.axis_index("rcv")
    core = lax.rem(cell, 2)
    yl = lax.rem(cell // 2, 2)
    x = lax.rem(cell // 4, 4)
    z = cell // 16

    def device(m1, m2, my, mc):
        z1, x1 = flip(z, m1), flip(x, m1)
        z2, x2 = flip(z, m2), flip(x, m2)
        zz = z2 + core * (z1 - z2)
        xx = x1 + core * (x2 - x1)
        yy = 1 - yl if my else yl
        cc = 1 - core if mc else core
        return (((zz * 4 + xx) * 2 + yy) * 2 + cc, rcv)

    sibling = device(0, 0, 0, 1)
    other = (cell, 1 - rcv)
    ring = [None] + [device(m, 0, 0, 0) for m in (1, 2, 3)]
    pairs = [None] + [device(0, m // 2, m % 2, 0) for m in range(1, 8)]

    loads = []
    for k in range(NKB):
        cells = pl.ds(k * KB, KB)
        loads.append(pltpu.make_async_copy(field.at[cells, :], fraw.at[cells, :], lsem.at[2 * k]))
        loads.append(pltpu.make_async_copy(green.at[:, cells], graw.at[:, cells], lsem.at[2 * k + 1]))
    load_probe = pltpu.make_async_copy(probe, prb, lsem.at[2 * NKB])
    load_cov = pltpu.make_async_copy(cov, craw, lsem.at[2 * NKB + 1])
    load_probe.start()
    for c in loads:
        c.start()
    load_cov.start()

    barrier = pltpu.get_barrier_semaphore()
    partners = [sibling, other] + ring[1:] + pairs[1:]
    for d in partners:
        pl.semaphore_signal(barrier, inc=1, device_id=d, device_id_type=MESH)

    started = []
    counter = [0]

    def remote(src, dst, dev):
        n = counter[0]
        counter[0] += 1
        c = pltpu.make_async_remote_copy(src_ref=src, dst_ref=dst, send_sem=ssem.at[n], recv_sem=rsem.at[n],
                                         device_id=dev, device_id_type=MESH)
        c.start()
        started.append(c)
        return c

    place1 = [[flip(x if c == 0 else z, a) for a in range(4)] for c in range(2)]
    place2 = [[flip(z if c == 0 else x, a) for a in range(4)] for c in range(2)]
    place_y = [yl, 1 - yl]
    place_c = [core, 1 - core]

    load_probe.wait()
    for k in range(NKB):
        cells = slice(k * KB, (k + 1) * KB)
        loads[2 * k].wait()
        turned = fraw[cells, :].T
        for c in range(2):
            for a1 in range(4):
                for a2 in range(4):
                    for y in range(2):
                        g = ((c * 4 + a1) * 4 + a2) * 2 + y
                        slot = ((place_c[c] * 4 + place1[c][a1]) * 4 + place2[c][a2]) * 2 + place_y[y]
                        ft[pl.ds(pl.multiple_of(slot * 8, 8), 8), cells] = turned[g * 8:(g + 1) * 8, :]
        loads[2 * k + 1].wait()
        ghi[:, cells], glo[:, cells] = split(graw[:, cells])

    waits = {}

    def forward(p, half):
        rows = slice(half * 256, half * 256 + 256)

        def step(k, _):
            cells = pl.ds(pl.multiple_of(k * KB, KB), KB)
            hi, lo = split(ft[rows, cells] * prb[p:p + 1, cells])
            part = nt(hi, ghi[:, cells]) + nt(hi, glo[:, cells]) + nt(lo, ghi[:, cells])

            @pl.when(k == 0)
            def _():
                data[p, rows] = part

            @pl.when(k > 0)
            def _():
                data[p, rows] += part

            return 0

        lax.fori_loop(0, NKB, step, 0)

    def whiten(p):
        waits["R", p].wait_recv()
        total = jnp.zeros((8, R), F32)
        for mine, vals in ((True, own[p]), (False, far[p])):
            hi, lo = split(vals)
            both = jnp.concatenate([hi, lo], axis=0)
            start = pl.multiple_of((rcv if mine else 1 - rcv) * R, R)
            a = nt(both, chi[:, pl.ds(start, R)])
            b = nt(both, clo[:, pl.ds(start, R)])
            total += (a[:8] + a[8:]) + (b[:8] + b[8:])
        white[p, 0:8] = total

    def backward(p, half):
        rows = slice(half * 256, half * 256 + 256)
        hi, lo = split(white[p, rows])

        def step(n, _):
            cells = pl.ds(pl.multiple_of(n * NB, NB), NB)
            g, l = ghi[:, cells], glo[:, cells]
            back = nn(hi, g) + nn(hi, l) + nn(lo, g)
            part = jnp.sum(back * ft[rows, cells], axis=0, keepdims=True)
            if half == 0:
                hess[p, :, cells] = part
            else:
                hess[p, :, cells] += part
            return 0

        lax.fori_loop(0, NNB, step, 0)

    first = [True]
    for word in order:
        op, _, p = word.partition(".")
        p = int(p) if p else 0
        if op == "F1":
            forward(p, 1)
            if first[0]:
                pl.semaphore_wait(barrier, len(partners))
                first[0] = False
            waits["C", p] = [remote(data.at[p, pl.ds(256, 256)], core_in.at[p], sibling)]
        elif op == "F0":
            forward(p, 0)
        elif op == "C":
            waits["C", p][0].wait_recv()
            data[p, 0:256] += core_in[p]
            waits["A", p] = [remote(data.at[p, pl.ds(64 * m, 64)], ring_in.at[p, m - 1], ring[m]) for m in (2, 1, 3)]
        elif op == "A":
            for c in waits["A", p]:
                c.wait_recv()
            data[p, 0:64] = (data[p, 0:64] + ring_in[p, 0]) + (ring_in[p, 1] + ring_in[p, 2])
            waits["Y", p] = [remote(data.at[p, pl.ds(8 * m, 8)], pair_in.at[p, m - 1], pairs[m])
                             for m in (5, 4, 7, 3, 6, 2, 1)]
            if p == 0:
                load_cov.wait()
                chi[...], clo[...] = split(craw[...])
        elif op == "Y":
            for c in waits["Y", p]:
                c.wait_recv()
            total = data[p, 0:8]
            for m in range(7):
                total += pair_in[p, m]
            own[p] = total
            waits["R", p] = remote(own.at[p], far.at[p], other)
        elif op == "R":
            whiten(p)
            waits["V", p] = [remote(white.at[p, pl.ds(0, 8)], white.at[p, pl.ds(8 * m, 8)], pairs[m])
                             for m in (5, 4, 7, 3, 6, 2, 1)]
        elif op == "V":
            for c in waits["V", p]:
                c.wait_recv()
            waits["U", p] = [remote(white.at[p, pl.ds(0, 64)], white.at[p, pl.ds(64 * m, 64)], ring[m])
                             for m in (2, 1, 3)]
        elif op == "U":
            for c in waits["U", p]:
                c.wait_recv()
            waits["S", p] = remote(white.at[p, pl.ds(0, 256)], white.at[p, pl.ds(256, 256)], sibling)
        elif op == "B0":
            backward(p, 0)
        elif op == "B1":
            waits["S", p].wait_recv()
            backward(p, 1)
            waits["H", p] = remote(hess.at[p], hr_out.at[p], other)
        elif op == "G0":
            for a in range(NP):
                for b in range(NP):
                    t = jnp.sum(own[a] * white[b, 0:8], axis=0, keepdims=True)
                    gram[a * NP + b:a * NP + b + 1, :] = (t[:, 0:128] + t[:, 128:256]) + (t[:, 256:384] + t[:, 384:])
            waits["G"] = [remote(gram, g8.at[m - 1], pairs[m]) for m in range(1, 8)]
        elif op == "G1":
            for c in waits["G"]:
                c.wait_recv()
            total = gram[...]
            for m in range(7):
                total += g8[m]
            g1[0] = total
            waits["G"] = [remote(g1.at[0], g4.at[m - 1], ring[m]) for m in (1, 2, 3)]
        elif op == "G2":
            for c in waits["G"]:
                c.wait_recv()
            g1[1] = (g1[0] + g4[0]) + (g4[1] + g4[2])
            waits["G"] = [remote(g1.at[1], g2.at[0], sibling)]
        elif op == "G3":
            waits["G"][0].wait_recv()
            g1[2] = g1[1] + g2[0]
            waits["G"] = [remote(g1.at[2], g2.at[1], other)]
    for p in range(NP):
        if ("H", p) in waits:
            waits["H", p].wait_recv()
        h_out[p] = hess[p]
    waits["G"][0].wait_recv()
    g_out[...] = g1[2] + g2[1]
    for c in started:
        c.wait_send()


def local(green, field, probe, cov):
    any_spec = pl.BlockSpec(memory_space=pl.ANY)
    vmem = pl.BlockSpec(memory_space=pltpu.VMEM)
    n_remote = NP * 24 + 12
    h, hr, g = pl.pallas_call(
        functools.partial(kernel, ORDER),
        name="probes",
        out_shape=(jax.ShapeDtypeStruct((NP, 1, C), F32), jax.ShapeDtypeStruct((NP, 1, C), F32),
                   jax.ShapeDtypeStruct((16, 128), F32)),
        in_specs=[any_spec] * 4,
        out_specs=(vmem, vmem, vmem),
        scratch_shapes=[
            pltpu.VMEM((R, C), F32),
            pltpu.VMEM((C, S), F32),
            pltpu.VMEM((R, 2 * R), F32),
            pltpu.VMEM((NP, C), F32),
            pltpu.VMEM((R, C), BF16),
            pltpu.VMEM((R, C), BF16),
            pltpu.VMEM((S, C), F32),
            pltpu.VMEM((R, 2 * R), BF16),
            pltpu.VMEM((R, 2 * R), BF16),
            pltpu.VMEM((NP, S, R), F32),
            pltpu.VMEM((NP, 256, R), F32),
            pltpu.VMEM((NP, 3, 64, R), F32),
            pltpu.VMEM((NP, 7, 8, R), F32),
            pltpu.VMEM((NP, 8, R), F32),
            pltpu.VMEM((NP, 8, R), F32),
            pltpu.VMEM((NP, S, R), F32),
            pltpu.VMEM((NP, 1, C), F32),
            pltpu.VMEM((16, 128), F32),
            pltpu.VMEM((7, 16, 128), F32),
            pltpu.VMEM((3, 16, 128), F32),
            pltpu.VMEM((2, 16, 128), F32),
            pltpu.VMEM((3, 16, 128), F32),
            pltpu.SemaphoreType.DMA((2 * NKB + 2,)),
            pltpu.SemaphoreType.DMA((n_remote,)),
            pltpu.SemaphoreType.DMA((n_remote,)),
        ],
        compiler_params=pltpu.CompilerParams(collective_id=0, has_side_effects=True, vmem_limit_bytes=56 * 2 ** 20),
        cost_estimate=pl.CostEstimate(flops=6 * 2 * R * C * S * NP, bytes_accessed=10 * 2 ** 20, transcendentals=0),
    )(green, field, probe, cov)
    hessian = (h + hr).reshape(NP, C)
    curvature = jnp.sum(g, axis=1).reshape(NP, NP) / (1024 * S)
    return hessian, curvature


def solution(mesh):
    return jax.shard_map(
        local,
        mesh=mesh,
        in_specs=(P("rcv", "cell"), P("cell", None), P(None, "cell"), P("rcv", None)),
        out_specs=(P(None, "cell"), P()),
        check_vma=False,
    )
```

```python
import functools

import jax
import jax.numpy as jnp
from jax import lax
from jax.experimental import pallas as pl
from jax.experimental.pallas import tpu as pltpu
from jax.sharding import PartitionSpec as P

MESH = pl.DeviceIdType.MESH
F32 = jnp.float32
BF16 = jnp.bfloat16
NP = 4
S = 512
R = 512
C = 2048
KB = 512
NKB = C // KB
NB = 512
NNB = C // NB

ORDER = [
    "F1a.0", "F1b.0", "F0a.0", "F0b.0", "F1a.1", "C.0", "F1b.1", "F0a.1", "F0b.1", "F1a.2", "C.1", "F1b.2",
    "F0a.2", "F0b.2", "A.0", "F1a.3", "C.2", "F1b.3", "F0a.3", "F0b.3", "A.1", "C.3", "R.0", "A.2", "R.1",
    "A.3", "V.0", "R.2", "V.1", "U.0", "B0a.0", "R.3", "V.2", "B0b.0", "G0", "U.1", "B1a.0", "B1b.0",
    "B0a.1", "V.3", "B0b.1", "B1a.1", "U.2", "B1b.1", "G1", "B0a.2", "B0b.2", "B1a.2", "U.3", "B1b.2",
    "B0a.3", "B0b.3", "G2", "B1a.3", "B1b.3", "G3",
]


def flip(v, m):
    if m == 0:
        return v
    if m == 1:
        return v + 1 - 2 * lax.rem(v, 2)
    if m == 2:
        return lax.rem(v + 2, 4)
    return 3 - v


def split(a):
    hi = a.astype(BF16)
    return hi, (a - hi.astype(F32)).astype(BF16)


def nt(a, b):
    return lax.dot_general(a, b, (((1,), (1,)), ((), ())), preferred_element_type=F32)


def nn(a, b):
    return lax.dot_general(a, b, (((1,), (0,)), ((), ())), preferred_element_type=F32)


def kernel(order, green, field, probe, cov, h_out, g_out,
           graw, fraw, craw, prb, ghi, glo, ft, chi, clo, data, core_in, ring_in, pair_in, own, white, hess, hess_in,
           gram, g8, g4, g2, g1, lsem, ssem, rsem):
    cell = lax.axis_index("cell")
    rcv = lax.axis_index("rcv")
    core = lax.rem(cell, 2)
    yl = lax.rem(cell // 2, 2)
    x = lax.rem(cell // 4, 4)
    z = cell // 16

    def device(m1, m2, my, mc, mr=0):
        z1, x1 = flip(z, m1), flip(x, m1)
        z2, x2 = flip(z, m2), flip(x, m2)
        zz = z2 + core * (z1 - z2)
        xx = x1 + core * (x2 - x1)
        yy = 1 - yl if my else yl
        cc = 1 - core if mc else core
        return (((zz * 4 + xx) * 2 + yy) * 2 + cc, 1 - rcv if mr else rcv)

    sibling = device(0, 0, 0, 1)
    other = device(0, 0, 0, 0, 1)
    facing = [device(0, m // 2, m % 2, 0, 1) for m in range(8)]
    ring = [None] + [device(m, 0, 0, 0) for m in (1, 2, 3)]
    pairs = [None] + [device(0, m // 2, m % 2, 0) for m in range(1, 8)]

    loads = []
    for k in range(NKB):
        cells = pl.ds(k * KB, KB)
        loads.append(pltpu.make_async_copy(field.at[cells, :], fraw.at[cells, :], lsem.at[2 * k]))
        loads.append(pltpu.make_async_copy(green.at[:, cells], graw.at[:, cells], lsem.at[2 * k + 1]))
    load_probe = pltpu.make_async_copy(probe, prb, lsem.at[2 * NKB])
    load_cov = pltpu.make_async_copy(cov, craw, lsem.at[2 * NKB + 1])
    load_probe.start()
    for c in loads:
        c.start()
    load_cov.start()

    barrier = pltpu.get_barrier_semaphore()
    partners = [sibling] + facing + ring[1:] + pairs[1:]
    for d in partners:
        pl.semaphore_signal(barrier, inc=1, device_id=d, device_id_type=MESH)

    started = []
    counter = [0]

    def remote(src, dst, dev):
        n = counter[0]
        counter[0] += 1
        c = pltpu.make_async_remote_copy(src_ref=src, dst_ref=dst, send_sem=ssem.at[n], recv_sem=rsem.at[n],
                                         device_id=dev, device_id_type=MESH)
        c.start()
        started.append(c)
        return c

    place1 = [[flip(x if c == 0 else z, a) for a in range(4)] for c in range(2)]
    place2 = [[flip(z if c == 0 else x, a) for a in range(4)] for c in range(2)]
    place_y = [yl, 1 - yl]
    place_c = [core, 1 - core]

    load_probe.wait()
    for k in range(NKB):
        cells = slice(k * KB, (k + 1) * KB)
        loads[2 * k].wait()
        turned = fraw[cells, :].T
        for c in range(2):
            for a1 in range(4):
                for a2 in range(4):
                    for y in range(2):
                        g = ((c * 4 + a1) * 4 + a2) * 2 + y
                        slot = ((place_c[c] * 4 + place1[c][a1]) * 4 + place2[c][a2]) * 2 + place_y[y]
                        ft[pl.ds(pl.multiple_of(slot * 8, 8), 8), cells] = turned[g * 8:(g + 1) * 8, :]
        loads[2 * k + 1].wait()
        ghi[:, cells], glo[:, cells] = split(graw[:, cells])

    waits = {}

    def forward(p, half, part_at):
        rows = slice(half * 256, half * 256 + 256)

        total = data[p, rows] if part_at else None
        for k in range(part_at * NKB // 2, (part_at + 1) * NKB // 2):
            cells = slice(k * KB, (k + 1) * KB)
            hi, lo = split(ft[rows, cells] * prb[p:p + 1, cells])
            part = nt(hi, ghi[:, cells]) + nt(hi, glo[:, cells]) + nt(lo, ghi[:, cells])
            total = part if total is None else total + part
        data[p, rows] = total

    def whiten(p):
        for c in waits["R", p]:
            c.wait_recv()
        near, away = data[p, 0:8], pair_in[p, 7]
        for m in range(7):
            near += pair_in[p, m]
            away += pair_in[p, 8 + m]
        own[p] = near
        total = jnp.zeros((8, R), F32)
        for mine, vals in ((True, near), (False, away)):
            hi, lo = split(vals)
            both = jnp.concatenate([hi, lo], axis=0)
            start = pl.multiple_of((rcv if mine else 1 - rcv) * R, R)
            a = nt(both, chi[:, pl.ds(start, R)])
            b = nt(both, clo[:, pl.ds(start, R)])
            total += (a[:8] + a[8:]) + (b[:8] + b[8:])
        white[p, 0:8] = total

    def backward(p, half, part_at):
        rows = slice(half * 256, half * 256 + 256)
        hi, lo = split(white[p, rows])

        for n in range(part_at * NNB // 2, (part_at + 1) * NNB // 2):
            cells = slice(n * NB, (n + 1) * NB)
            g, l = ghi[:, cells], glo[:, cells]
            back = nn(hi, g) + nn(hi, l) + nn(lo, g)
            part = jnp.sum(back * ft[rows, cells], axis=0, keepdims=True)
            if half == 0:
                hess[p, :, cells] = part
            else:
                hess[p, :, cells] += part

    first = [True]
    for word in order:
        op, _, p = word.partition(".")
        p = int(p) if p else 0
        if op == "F1a":
            forward(p, 1, 0)
        elif op == "F1b":
            forward(p, 1, 1)
            if first[0]:
                pl.semaphore_wait(barrier, len(partners))
                first[0] = False
            waits["C", p] = [remote(data.at[p, pl.ds(256, 256)], core_in.at[p], sibling)]
        elif op == "F0a":
            forward(p, 0, 0)
        elif op == "F0b":
            forward(p, 0, 1)
        elif op == "C":
            waits["C", p][0].wait_recv()
            data[p, 0:256] += core_in[p]
            waits["A", p] = [remote(data.at[p, pl.ds(64 * m, 64)], ring_in.at[p, m - 1], ring[m]) for m in (2, 1, 3)]
        elif op == "A":
            for c in waits["A", p]:
                c.wait_recv()
            data[p, 0:64] = (data[p, 0:64] + ring_in[p, 0]) + (ring_in[p, 1] + ring_in[p, 2])
            waits["R", p] = [remote(data.at[p, pl.ds(8 * m, 8)], pair_in.at[p, n], dev) for m, n, dev in
                             [(m, 7 + m, facing[m]) for m in (5, 4, 7, 3, 6, 2, 1, 0)]
                             + [(m, m - 1, pairs[m]) for m in (5, 4, 7, 3, 6, 2, 1)]]
            if p == 0:
                load_cov.wait()
                chi[...], clo[...] = split(craw[...])
        elif op == "R":
            whiten(p)
            waits["V", p] = [remote(white.at[p, pl.ds(0, 8)], white.at[p, pl.ds(8 * m, 8)], pairs[m])
                             for m in (5, 4, 7, 3, 6, 2, 1)]
        elif op == "V":
            for c in waits["V", p]:
                c.wait_recv()
            waits["U", p] = [remote(white.at[p, pl.ds(0, 64)], white.at[p, pl.ds(64 * m, 64)], ring[m])
                             for m in (2, 1, 3)]
        elif op == "U":
            for c in waits["U", p]:
                c.wait_recv()
            waits["S", p] = remote(white.at[p, pl.ds(0, 256)], white.at[p, pl.ds(256, 256)], sibling)
        elif op == "B0a":
            backward(p, 0, 0)
        elif op == "B0b":
            backward(p, 0, 1)
        elif op == "B1a":
            waits["S", p].wait_recv()
            backward(p, 1, 0)
        elif op == "B1b":
            backward(p, 1, 1)
            waits["H", p] = remote(hess.at[p], hess_in.at[p], other)
        elif op == "G0":
            for a in range(NP):
                for b in range(NP):
                    t = jnp.sum(own[a] * white[b, 0:8], axis=0, keepdims=True)
                    gram[a * NP + b:a * NP + b + 1, :] = (t[:, 0:128] + t[:, 128:256]) + (t[:, 256:384] + t[:, 384:])
            waits["G"] = [remote(gram, g8.at[m - 1], pairs[m]) for m in range(1, 8)]
        elif op == "G1":
            for c in waits["G"]:
                c.wait_recv()
            total = gram[...]
            for m in range(7):
                total += g8[m]
            g1[0] = total
            waits["G"] = [remote(g1.at[0], g4.at[m - 1], ring[m]) for m in (1, 2, 3)]
        elif op == "G2":
            for c in waits["G"]:
                c.wait_recv()
            g1[1] = (g1[0] + g4[0]) + (g4[1] + g4[2])
            waits["G"] = [remote(g1.at[1], g2.at[0], sibling)]
        elif op == "G3":
            waits["G"][0].wait_recv()
            g1[2] = g1[1] + g2[0]
            waits["G"] = [remote(g1.at[2], g2.at[1], other)]
    for p in range(NP):
        waits["H", p].wait_recv()
        h_out[p:p + 1, :] = hess[p] + hess_in[p]
    waits["G"][0].wait_recv()
    sums = jnp.sum(g1[2] + g2[1], axis=1, keepdims=True) * (1.0 / (2 * R * S))
    for a in range(NP):
        for b in range(NP):
            g_out[a:a + 1, b:b + 1] = sums[a * NP + b:a * NP + b + 1, :]
    for c in started:
        c.wait_send()


def local(green, field, probe, cov):
    any_spec = pl.BlockSpec(memory_space=pl.ANY)
    vmem = pl.BlockSpec(memory_space=pltpu.VMEM)
    n_remote = NP * 32 + 12
    return pl.pallas_call(
        functools.partial(kernel, ORDER),
        name="probes",
        out_shape=(jax.ShapeDtypeStruct((NP, C), F32), jax.ShapeDtypeStruct((NP, NP), F32)),
        in_specs=[any_spec] * 4,
        out_specs=(vmem, vmem),
        scratch_shapes=[
            pltpu.VMEM((R, C), F32),
            pltpu.VMEM((C, S), F32),
            pltpu.VMEM((R, 2 * R), F32),
            pltpu.VMEM((NP, C), F32),
            pltpu.VMEM((R, C), BF16),
            pltpu.VMEM((R, C), BF16),
            pltpu.VMEM((S, C), F32),
            pltpu.VMEM((R, 2 * R), BF16),
            pltpu.VMEM((R, 2 * R), BF16),
            pltpu.VMEM((NP, S, R), F32),
            pltpu.VMEM((NP, 256, R), F32),
            pltpu.VMEM((NP, 3, 64, R), F32),
            pltpu.VMEM((NP, 15, 8, R), F32),
            pltpu.VMEM((NP, 8, R), F32),
            pltpu.VMEM((NP, S, R), F32),
            pltpu.VMEM((NP, 1, C), F32),
            pltpu.VMEM((NP, 1, C), F32),
            pltpu.VMEM((16, 128), F32),
            pltpu.VMEM((7, 16, 128), F32),
            pltpu.VMEM((3, 16, 128), F32),
            pltpu.VMEM((2, 16, 128), F32),
            pltpu.VMEM((3, 16, 128), F32),
            pltpu.SemaphoreType.DMA((2 * NKB + 2,)),
            pltpu.SemaphoreType.DMA((n_remote,)),
            pltpu.SemaphoreType.DMA((n_remote,)),
        ],
        compiler_params=pltpu.CompilerParams(collective_id=0, has_side_effects=True, vmem_limit_bytes=56 * 2 ** 20),
        cost_estimate=pl.CostEstimate(flops=6 * 2 * R * C * S * NP, bytes_accessed=10 * 2 ** 20, transcendentals=0),
    )(green, field, probe, cov)


def solution(mesh):
    return jax.shard_map(
        local,
        mesh=mesh,
        in_specs=(P("rcv", "cell"), P("cell", None), P(None, "cell"), P("rcv", None)),
        out_specs=(P(None, "cell"), P()),
        check_vma=False,
    )
```

```python
import functools

import jax
import jax.numpy as jnp
from jax import lax
from jax.experimental import pallas as pl
from jax.experimental.pallas import tpu as pltpu
from jax.sharding import PartitionSpec as P

MESH = pl.DeviceIdType.MESH
F32 = jnp.float32
BF16 = jnp.bfloat16
NP = 4
S = 512
R = 512
C = 2048
KB = 512
NKB = C // KB
NB = 512
NNB = C // NB

ORDER = [
    "P.0", "P.1", "F1a.0", "P.2", "P.3", "F1b.0", "F0a.0", "F0b.0", "F1a.1", "C.0", "F1b.1", "F0a.1",
    "F0b.1", "F1a.2", "C.1", "F1b.2", "F0a.2", "A.0", "F0b.2", "F1a.3", "C.2", "F1b.3", "A.1", "F0a.3",
    "F0b.3", "C.3", "R.0", "A.2", "R.1", "V.0", "A.3", "R.2", "V.1", "U.0", "B0a.0", "B0b.0", "R.3", "V.2",
    "G0", "B1a.0", "U.1", "B1b.0", "B0a.1", "V.3", "B0b.1", "B1a.1", "U.2", "G1", "B1b.1", "B0a.2", "B0b.2",
    "U.3", "B1a.2", "B1b.2", "G2", "B0a.3", "B0b.3", "B1a.3", "B1b.3", "G3",
]


def flip(v, m):
    if m == 0:
        return v
    if m == 1:
        return v + 1 - 2 * lax.rem(v, 2)
    if m == 2:
        return lax.rem(v + 2, 4)
    return 3 - v


def split(a):
    hi = a.astype(BF16)
    return hi, (a - hi.astype(F32)).astype(BF16)


def nt(a, b):
    return lax.dot_general(a, b, (((1,), (1,)), ((), ())), preferred_element_type=F32)


def nn(a, b):
    return lax.dot_general(a, b, (((1,), (0,)), ((), ())), preferred_element_type=F32)


def kernel(order, green, field, probe, cov, h_out, away_out, g_out,
           graw, fraw, craw, prb, ghi, glo, ft, chi, clo, data, core_in, ring_in, pair_in, own, white, hess, hess_in,
           gram, g16, g4, g2, g1, lsem, ssem, rsem):
    cell = lax.axis_index("cell")
    rcv = lax.axis_index("rcv")
    core = lax.rem(cell, 2)
    yl = lax.rem(cell // 2, 2)
    x = lax.rem(cell // 4, 4)
    z = cell // 16

    def device(m1, m2, my, mc, mr=0):
        z1, x1 = flip(z, m1), flip(x, m1)
        z2, x2 = flip(z, m2), flip(x, m2)
        zz = z2 + core * (z1 - z2)
        xx = x1 + core * (x2 - x1)
        yy = 1 - yl if my else yl
        cc = 1 - core if mc else core
        return (((zz * 4 + xx) * 2 + yy) * 2 + cc, 1 - rcv if mr else rcv)

    sibling = device(0, 0, 0, 1)
    other = device(0, 0, 0, 0, 1)
    facing = [device(0, m // 2, m % 2, 0, 1) for m in range(8)]
    ring = [None] + [device(m, 0, 0, 0) for m in (1, 2, 3)]
    pairs = [None] + [device(0, m // 2, m % 2, 0) for m in range(1, 8)]

    loads = []
    for k in range(NKB):
        cells = pl.ds(k * KB, KB)
        loads.append(pltpu.make_async_copy(field.at[cells, :], fraw.at[cells, :], lsem.at[2 * k]))
        loads.append(pltpu.make_async_copy(green.at[:, cells], graw.at[:, cells], lsem.at[2 * k + 1]))
    load_probe = pltpu.make_async_copy(probe, prb, lsem.at[2 * NKB])
    load_cov = pltpu.make_async_copy(cov, craw, lsem.at[2 * NKB + 1])
    load_probe.start()
    for c in loads:
        c.start()
    load_cov.start()

    barrier = pltpu.get_barrier_semaphore()
    partners = [sibling] + facing + ring[1:] + pairs[1:]
    for d in partners:
        pl.semaphore_signal(barrier, inc=1, device_id=d, device_id_type=MESH)

    started = []
    counter = [0]

    def remote(src, dst, dev):
        n = counter[0]
        counter[0] += 1
        c = pltpu.make_async_remote_copy(src_ref=src, dst_ref=dst, send_sem=ssem.at[n], recv_sem=rsem.at[n],
                                         device_id=dev, device_id_type=MESH)
        c.start()
        started.append(c)
        return c

    place1 = [[flip(x if c == 0 else z, a) for a in range(4)] for c in range(2)]
    place2 = [[flip(z if c == 0 else x, a) for a in range(4)] for c in range(2)]
    place_y = [yl, 1 - yl]
    place_c = [core, 1 - core]

    load_probe.wait()

    def prepare(k):
        cells = slice(k * KB, (k + 1) * KB)
        loads[2 * k].wait()
        turned = fraw[cells, :].T
        for c in range(2):
            for a1 in range(4):
                for a2 in range(4):
                    for y in range(2):
                        g = ((c * 4 + a1) * 4 + a2) * 2 + y
                        slot = ((place_c[c] * 4 + place1[c][a1]) * 4 + place2[c][a2]) * 2 + place_y[y]
                        ft[pl.ds(pl.multiple_of(slot * 8, 8), 8), cells] = turned[g * 8:(g + 1) * 8, :]
        loads[2 * k + 1].wait()
        ghi[:, cells], glo[:, cells] = split(graw[:, cells])

    waits = {}

    def forward(p, half, part_at):
        rows = slice(half * 256, half * 256 + 256)

        total = data[p, rows] if part_at else None
        for k in range(part_at * NKB // 2, (part_at + 1) * NKB // 2):
            cells = slice(k * KB, (k + 1) * KB)
            hi, lo = split(ft[rows, cells] * prb[p:p + 1, cells])
            part = nt(hi, ghi[:, cells]) + nt(hi, glo[:, cells]) + nt(lo, ghi[:, cells])
            total = part if total is None else total + part
        data[p, rows] = total

    def whiten(p):
        for c in waits["R", p]:
            c.wait_recv()
        near, away = data[p, 0:8], pair_in[p, 7]
        for m in range(7):
            near += pair_in[p, m]
            away += pair_in[p, 8 + m]
        own[p] = near
        total = jnp.zeros((8, R), F32)
        for mine, vals in ((True, near), (False, away)):
            hi, lo = split(vals)
            both = jnp.concatenate([hi, lo], axis=0)
            start = pl.multiple_of((rcv if mine else 1 - rcv) * R, R)
            a = nt(both, chi[:, pl.ds(start, R)])
            b = nt(both, clo[:, pl.ds(start, R)])
            total += (a[:8] + a[8:]) + (b[:8] + b[8:])
        white[p, 0:8] = total

    def backward(p, half, part_at):
        rows = slice(half * 256, half * 256 + 256)
        hi, lo = split(white[p, rows])

        for n in range(part_at * NNB // 2, (part_at + 1) * NNB // 2):
            cells = slice(n * NB, (n + 1) * NB)
            g, l = ghi[:, cells], glo[:, cells]
            back = nn(hi, g) + nn(hi, l) + nn(lo, g)
            part = jnp.sum(back * ft[rows, cells], axis=0, keepdims=True)
            if half == 0:
                hess[p, :, cells] = part
            else:
                hess[p, :, cells] += part

    first = [True]
    for word in order:
        op, _, p = word.partition(".")
        p = int(p) if p else 0
        if op == "P":
            prepare(p)
        elif op == "F1a":
            forward(p, 1, 0)
        elif op == "F1b":
            forward(p, 1, 1)
            if first[0]:
                pl.semaphore_wait(barrier, len(partners))
                first[0] = False
            waits["C", p] = [remote(data.at[p, pl.ds(256, 256)], core_in.at[p], sibling)]
        elif op == "F0a":
            forward(p, 0, 0)
        elif op == "F0b":
            forward(p, 0, 1)
        elif op == "C":
            waits["C", p][0].wait_recv()
            data[p, 0:256] += core_in[p]
            waits["A", p] = [remote(data.at[p, pl.ds(64 * m, 64)], ring_in.at[p, m - 1], ring[m]) for m in (2, 1, 3)]
        elif op == "A":
            for c in waits["A", p]:
                c.wait_recv()
            data[p, 0:64] = (data[p, 0:64] + ring_in[p, 0]) + (ring_in[p, 1] + ring_in[p, 2])
            waits["R", p] = [remote(data.at[p, pl.ds(8 * m, 8)], pair_in.at[p, n], dev) for m, n, dev in
                             [(m, 7 + m, facing[m]) for m in (5, 4, 7, 3, 6, 2, 1, 0)]
                             + [(m, m - 1, pairs[m]) for m in (5, 4, 7, 3, 6, 2, 1)]]
            if p == 0:
                load_cov.wait()
                chi[...], clo[...] = split(craw[...])
        elif op == "R":
            whiten(p)
            waits["V", p] = [remote(white.at[p, pl.ds(0, 8)], white.at[p, pl.ds(8 * m, 8)], pairs[m])
                             for m in (5, 4, 7, 3, 6, 2, 1)]
        elif op == "V":
            for c in waits["V", p]:
                c.wait_recv()
            waits["U", p] = [remote(white.at[p, pl.ds(0, 64)], white.at[p, pl.ds(64 * m, 64)], ring[m])
                             for m in (2, 1, 3)]
        elif op == "U":
            for c in waits["U", p]:
                c.wait_recv()
            waits["S", p] = remote(white.at[p, pl.ds(0, 256)], white.at[p, pl.ds(256, 256)], sibling)
        elif op == "B0a":
            backward(p, 0, 0)
        elif op == "B0b":
            backward(p, 0, 1)
        elif op == "B1a":
            waits["S", p].wait_recv()
            backward(p, 1, 0)
        elif op == "B1b":
            backward(p, 1, 1)
            h_out[p:p + 1, :] = hess[p]
            waits["H", p] = remote(hess.at[p], hess_in.at[p], other)
        elif op == "G0":
            for a in range(NP):
                for b in range(NP):
                    t = jnp.sum(own[a] * white[b, 0:8], axis=0, keepdims=True)
                    gram[a * NP + b:a * NP + b + 1, :] = (t[:, 0:128] + t[:, 128:256]) + (t[:, 256:384] + t[:, 384:])
            waits["G"] = [remote(gram, g16.at[n], dev) for n, dev in enumerate(facing + pairs[1:])]
        elif op == "G1":
            for c in waits["G"]:
                c.wait_recv()
            total = gram[...]
            for m in range(15):
                total += g16[m]
            g1[0] = total
            waits["G"] = [remote(g1.at[0], g4.at[m - 1], ring[m]) for m in (1, 2, 3)]
        elif op == "G2":
            for c in waits["G"]:
                c.wait_recv()
            g1[1] = (g1[0] + g4[0]) + (g4[1] + g4[2])
            waits["G"] = [remote(g1.at[1], g2, sibling)]
        elif op == "G3":
            waits["G"][0].wait_recv()
            sums = jnp.sum(g1[1] + g2[...], axis=1, keepdims=True)
            for a in range(NP):
                for b in range(NP):
                    g_out[a:a + 1, b:b + 1] = sums[a * NP + b:a * NP + b + 1, :]
    for p in range(NP):
        waits["H", p].wait_recv()
        away_out[p:p + 1, :] = hess_in[p]
    for c in started:
        c.wait_send()


def local(green, field, probe, cov):
    any_spec = pl.BlockSpec(memory_space=pl.ANY)
    vmem = pl.BlockSpec(memory_space=pltpu.VMEM)
    n_remote = NP * 32 + 20
    mine, away, sums = pl.pallas_call(
        functools.partial(kernel, ORDER),
        name="probes",
        out_shape=(jax.ShapeDtypeStruct((NP, C), F32), jax.ShapeDtypeStruct((NP, C), F32),
                   jax.ShapeDtypeStruct((NP, NP), F32)),
        in_specs=[any_spec] * 4,
        out_specs=(vmem, vmem, vmem),
        scratch_shapes=[
            pltpu.VMEM((R, C), F32),
            pltpu.VMEM((C, S), F32),
            pltpu.VMEM((R, 2 * R), F32),
            pltpu.VMEM((NP, C), F32),
            pltpu.VMEM((R, C), BF16),
            pltpu.VMEM((R, C), BF16),
            pltpu.VMEM((S, C), F32),
            pltpu.VMEM((R, 2 * R), BF16),
            pltpu.VMEM((R, 2 * R), BF16),
            pltpu.VMEM((NP, S, R), F32),
            pltpu.VMEM((NP, 256, R), F32),
            pltpu.VMEM((NP, 3, 64, R), F32),
            pltpu.VMEM((NP, 15, 8, R), F32),
            pltpu.VMEM((NP, 8, R), F32),
            pltpu.VMEM((NP, S, R), F32),
            pltpu.VMEM((NP, 1, C), F32),
            pltpu.VMEM((NP, 1, C), F32),
            pltpu.VMEM((16, 128), F32),
            pltpu.VMEM((15, 16, 128), F32),
            pltpu.VMEM((3, 16, 128), F32),
            pltpu.VMEM((16, 128), F32),
            pltpu.VMEM((2, 16, 128), F32),
            pltpu.SemaphoreType.DMA((2 * NKB + 2,)),
            pltpu.SemaphoreType.DMA((n_remote,)),
            pltpu.SemaphoreType.DMA((n_remote,)),
        ],
        compiler_params=pltpu.CompilerParams(collective_id=0, has_side_effects=True, vmem_limit_bytes=56 * 2 ** 20),
        cost_estimate=pl.CostEstimate(flops=6 * 2 * R * C * S * NP, bytes_accessed=10 * 2 ** 20, transcendentals=0),
    )(green, field, probe, cov)
    return mine + away, sums / (2 * R * S)


def solution(mesh):
    return jax.shard_map(
        local,
        mesh=mesh,
        in_specs=(P("rcv", "cell"), P("cell", None), P(None, "cell"), P("rcv", None)),
        out_specs=(P(None, "cell"), P()),
        check_vma=False,
    )
```

```python
import functools

import jax
import jax.numpy as jnp
from jax import lax
from jax.experimental import pallas as pl
from jax.experimental.pallas import tpu as pltpu
from jax.sharding import PartitionSpec as P

MESH = pl.DeviceIdType.MESH
F32 = jnp.float32
BF16 = jnp.bfloat16
NP = 4
S = 512
R = 512
C = 2048
KB = 512
NKB = C // KB
NB = 512
NNB = C // NB

ORDER = [
    "P.0", "P.1", "F1a.0", "P.2", "P.3", "F1b.0", "F0a.0", "F0b.0", "F1a.1", "C.0", "F1b.1", "F0a.1",
    "F0b.1", "F1a.2", "C.1", "F1b.2", "A.0", "F0a.2", "F0b.2", "F1a.3", "C.2", "F1b.3", "A.1", "F0a.3",
    "F0b.3", "R.0", "C.3", "A.2", "R.1", "V.0", "A.3", "R.2", "V.1", "U.0", "B0a.0", "B0b.0", "R.3", "V.2",
    "G0", "U.1", "B1a.0", "B1b.0", "B0a.1", "V.3", "B0b.1", "B1a.1", "U.2", "G1", "B1b.1", "B0a.2", "B0b.2",
    "U.3", "B1a.2", "B1b.2", "G2", "B0a.3", "B0b.3", "B1a.3", "B1b.3", "G3",
]


def flip(v, m):
    if m == 0:
        return v
    if m == 1:
        return v + 1 - 2 * lax.rem(v, 2)
    if m == 2:
        return lax.rem(v + 2, 4)
    return 3 - v


def split(a):
    hi = a.astype(BF16)
    return hi, (a - hi.astype(F32)).astype(BF16)


def nt(a, b):
    return lax.dot_general(a, b, (((1,), (1,)), ((), ())), preferred_element_type=F32)


def nn(a, b):
    return lax.dot_general(a, b, (((1,), (0,)), ((), ())), preferred_element_type=F32)


def kernel(order, green, field, probe, cov, h_out, away_out, g_out,
           graw, fraw, craw, prb, ghi, glo, ft, chi, clo, data, core_in, ring_in, pair_in, own, white, hess, hess_in,
           gram, g16, g4, g2, g1, lsem, ssem, rsem):
    cell = lax.axis_index("cell")
    rcv = lax.axis_index("rcv")
    core = lax.rem(cell, 2)
    yl = lax.rem(cell // 2, 2)
    x = lax.rem(cell // 4, 4)
    z = cell // 16

    def device(m1, m2, my, mc, mr=0):
        z1, x1 = flip(z, m1), flip(x, m1)
        z2, x2 = flip(z, m2), flip(x, m2)
        zz = z2 + core * (z1 - z2)
        xx = x1 + core * (x2 - x1)
        yy = 1 - yl if my else yl
        cc = 1 - core if mc else core
        return (((zz * 4 + xx) * 2 + yy) * 2 + cc, 1 - rcv if mr else rcv)

    sibling = device(0, 0, 0, 1)
    other = device(0, 0, 0, 0, 1)
    facing = [device(0, m // 2, m % 2, 0, 1) for m in range(8)]
    ring = [None] + [device(m, 0, 0, 0) for m in (1, 2, 3)]
    pairs = [None] + [device(0, m // 2, m % 2, 0) for m in range(1, 8)]

    loads = []
    for k in range(NKB):
        cells = pl.ds(k * KB, KB)
        loads.append(pltpu.make_async_copy(field.at[cells, :], fraw.at[cells, :], lsem.at[2 * k]))
        loads.append(pltpu.make_async_copy(green.at[:, cells], graw.at[:, cells], lsem.at[2 * k + 1]))
    load_probe = pltpu.make_async_copy(probe, prb, lsem.at[2 * NKB])
    load_cov = pltpu.make_async_copy(cov, craw, lsem.at[2 * NKB + 1])
    load_probe.start()
    for c in loads:
        c.start()
    load_cov.start()

    barrier = pltpu.get_barrier_semaphore()
    partners = [sibling] + facing + ring[1:] + pairs[1:]
    for d in partners:
        pl.semaphore_signal(barrier, inc=1, device_id=d, device_id_type=MESH)

    started = []
    counter = [0]

    def remote(src, dst, dev):
        n = counter[0]
        counter[0] += 1
        c = pltpu.make_async_remote_copy(src_ref=src, dst_ref=dst, send_sem=ssem.at[n], recv_sem=rsem.at[n],
                                         device_id=dev, device_id_type=MESH)
        c.start()
        started.append(c)
        return c

    place1 = [[flip(x if c == 0 else z, a) for a in range(4)] for c in range(2)]
    place2 = [[flip(z if c == 0 else x, a) for a in range(4)] for c in range(2)]
    place_y = [yl, 1 - yl]
    place_c = [core, 1 - core]

    load_probe.wait()

    def prepare(k):
        cells = slice(k * KB, (k + 1) * KB)
        loads[2 * k].wait()
        turned = fraw[cells, :].T
        for c in range(2):
            for a1 in range(4):
                for a2 in range(4):
                    for y in range(2):
                        g = ((c * 4 + a1) * 4 + a2) * 2 + y
                        slot = ((place_c[c] * 4 + place1[c][a1]) * 4 + place2[c][a2]) * 2 + place_y[y]
                        ft[pl.ds(pl.multiple_of(slot * 8, 8), 8), cells] = turned[g * 8:(g + 1) * 8, :]
        loads[2 * k + 1].wait()
        ghi[:, cells], glo[:, cells] = split(graw[:, cells])

    waits = {}

    def forward(p, half, part_at):
        rows = slice(half * 256, half * 256 + 256)

        total = data[p, rows] if part_at else None
        for k in range(part_at * NKB // 2, (part_at + 1) * NKB // 2):
            cells = slice(k * KB, (k + 1) * KB)
            hi, lo = split(ft[rows, cells] * prb[p:p + 1, cells])
            part = nt(hi, ghi[:, cells]) + nt(hi, glo[:, cells]) + nt(lo, ghi[:, cells])
            total = part if total is None else total + part
        data[p, rows] = total

    def whiten(p):
        for c in waits["R", p]:
            c.wait_recv()
        near, away = data[p, 0:8], pair_in[p, 7]
        for m in range(7):
            near += pair_in[p, m]
            away += pair_in[p, 8 + m]
        own[p] = near
        total = jnp.zeros((8, R), F32)
        for mine, vals in ((True, near), (False, away)):
            hi, lo = split(vals)
            both = jnp.concatenate([hi, lo], axis=0)
            start = pl.multiple_of((rcv if mine else 1 - rcv) * R, R)
            a = nt(both, chi[:, pl.ds(start, R)])
            b = nt(both, clo[:, pl.ds(start, R)])
            total += (a[:8] + a[8:]) + (b[:8] + b[8:])
        white[p, 0:8] = total

    def backward(p, half, part_at):
        rows = slice(half * 256, half * 256 + 256)
        hi, lo = split(white[p, rows])

        for n in range(part_at * NNB // 2, (part_at + 1) * NNB // 2):
            cells = slice(n * NB, (n + 1) * NB)
            g, l = ghi[:, cells], glo[:, cells]
            back = nn(hi, g) + nn(hi, l) + nn(lo, g)
            part = jnp.sum(back * ft[rows, cells], axis=0, keepdims=True)
            if half == 0:
                hess[p, :, cells] = part
            else:
                hess[p, :, cells] += part

    first = [True]
    for word in order:
        op, _, p = word.partition(".")
        p = int(p) if p else 0
        if op == "P":
            prepare(p)
        elif op == "F1a":
            forward(p, 1, 0)
        elif op == "F1b":
            forward(p, 1, 1)
            if first[0]:
                pl.semaphore_wait(barrier, len(partners))
                first[0] = False
            waits["C", p] = [remote(data.at[p, pl.ds(256, 256)], core_in.at[p], sibling)]
        elif op == "F0a":
            forward(p, 0, 0)
        elif op == "F0b":
            forward(p, 0, 1)
        elif op == "C":
            waits["C", p][0].wait_recv()
            data[p, 0:256] += core_in[p]
            waits["A", p] = [remote(data.at[p, pl.ds(64 * m, 64)], ring_in.at[p, m - 1], ring[m]) for m in (2, 1, 3)]
        elif op == "A":
            for c in waits["A", p]:
                c.wait_recv()
            data[p, 0:64] = (data[p, 0:64] + ring_in[p, 0]) + (ring_in[p, 1] + ring_in[p, 2])
            waits["R", p] = [remote(data.at[p, pl.ds(8 * m, 8)], pair_in.at[p, n], dev) for m, n, dev in
                             [(m, 7 + m, facing[m]) for m in (5, 4, 7, 3, 6, 2, 1, 0)]
                             + [(m, m - 1, pairs[m]) for m in (5, 4, 7, 3, 6, 2, 1)]]
            if p == 0:
                load_cov.wait()
                chi[...], clo[...] = split(craw[...])
        elif op == "R":
            whiten(p)
            waits["V", p] = [remote(white.at[p, pl.ds(0, 8)], white.at[p, pl.ds(8 * m, 8)], pairs[m])
                             for m in (5, 4, 7, 3, 6, 2, 1)]
        elif op == "V":
            for c in waits["V", p]:
                c.wait_recv()
            waits["U", p] = [remote(white.at[p, pl.ds(0, 64)], white.at[p, pl.ds(64 * m, 64)], ring[m])
                             for m in (2, 1, 3)]
        elif op == "U":
            for c in waits["U", p]:
                c.wait_recv()
            waits["S", p] = remote(white.at[p, pl.ds(0, 256)], white.at[p, pl.ds(256, 256)], sibling)
        elif op == "B0a":
            backward(p, 0, 0)
        elif op == "B0b":
            backward(p, 0, 1)
        elif op == "B1a":
            waits["S", p].wait_recv()
            backward(p, 1, 0)
        elif op == "B1b":
            backward(p, 1, 1)
            h_out[p:p + 1, :] = hess[p]
            waits["H", p] = remote(hess.at[p], hess_in.at[p], other)
        elif op == "G0":
            for a in range(NP):
                for b in range(NP):
                    t = jnp.sum(own[a] * white[b, 0:8], axis=0, keepdims=True)
                    gram[a * NP + b:a * NP + b + 1, :] = (t[:, 0:128] + t[:, 128:256]) + (t[:, 256:384] + t[:, 384:])
            waits["G"] = [remote(gram, g16.at[n], dev) for n, dev in enumerate(facing + pairs[1:])]
        elif op == "G1":
            for c in waits["G"]:
                c.wait_recv()
            total = gram[...]
            for m in range(15):
                total += g16[m]
            g1[0] = total
            waits["G"] = [remote(g1.at[0], g4.at[m - 1], ring[m]) for m in (1, 2, 3)]
        elif op == "G2":
            for c in waits["G"]:
                c.wait_recv()
            g1[1] = (g1[0] + g4[0]) + (g4[1] + g4[2])
            waits["G"] = [remote(g1.at[1], g2, sibling)]
        elif op == "G3":
            waits["G"][0].wait_recv()
            sums = jnp.sum(g1[1] + g2[...], axis=1, keepdims=True)
            for a in range(NP):
                for b in range(NP):
                    g_out[a:a + 1, b:b + 1] = sums[a * NP + b:a * NP + b + 1, :]
    for p in range(NP):
        waits["H", p].wait_recv()
        away_out[p:p + 1, :] = hess_in[p]
    for c in started:
        c.wait_send()


def local(green, field, probe, cov):
    any_spec = pl.BlockSpec(memory_space=pl.ANY)
    vmem = pl.BlockSpec(memory_space=pltpu.VMEM)
    n_remote = NP * 32 + 20
    mine, away, sums = pl.pallas_call(
        functools.partial(kernel, ORDER),
        name="probes",
        out_shape=(jax.ShapeDtypeStruct((NP, C), F32), jax.ShapeDtypeStruct((NP, C), F32),
                   jax.ShapeDtypeStruct((NP, NP), F32)),
        in_specs=[any_spec] * 4,
        out_specs=(vmem, vmem, vmem),
        scratch_shapes=[
            pltpu.VMEM((R, C), F32),
            pltpu.VMEM((C, S), F32),
            pltpu.VMEM((R, 2 * R), F32),
            pltpu.VMEM((NP, C), F32),
            pltpu.VMEM((R, C), BF16),
            pltpu.VMEM((R, C), BF16),
            pltpu.VMEM((S, C), F32),
            pltpu.VMEM((R, 2 * R), BF16),
            pltpu.VMEM((R, 2 * R), BF16),
            pltpu.VMEM((NP, S, R), F32),
            pltpu.VMEM((NP, 256, R), F32),
            pltpu.VMEM((NP, 3, 64, R), F32),
            pltpu.VMEM((NP, 15, 8, R), F32),
            pltpu.VMEM((NP, 8, R), F32),
            pltpu.VMEM((NP, S, R), F32),
            pltpu.VMEM((NP, 1, C), F32),
            pltpu.VMEM((NP, 1, C), F32),
            pltpu.VMEM((16, 128), F32),
            pltpu.VMEM((15, 16, 128), F32),
            pltpu.VMEM((3, 16, 128), F32),
            pltpu.VMEM((16, 128), F32),
            pltpu.VMEM((2, 16, 128), F32),
            pltpu.SemaphoreType.DMA((2 * NKB + 2,)),
            pltpu.SemaphoreType.DMA((n_remote,)),
            pltpu.SemaphoreType.DMA((n_remote,)),
        ],
        compiler_params=pltpu.CompilerParams(collective_id=0, has_side_effects=True, vmem_limit_bytes=56 * 2 ** 20),
        cost_estimate=pl.CostEstimate(flops=6 * 2 * R * C * S * NP, bytes_accessed=10 * 2 ** 20, transcendentals=0),
    )(green, field, probe, cov)
    return mine + away, sums / (2 * R * S)


def solution(mesh):
    return jax.shard_map(
        local,
        mesh=mesh,
        in_specs=(P("rcv", "cell"), P("cell", None), P(None, "cell"), P("rcv", None)),
        out_specs=(P(None, "cell"), P()),
        check_vma=False,
    )
```
